512 devices in a mesh: row: 32 (over z, x), col: 16 (over y, core).
Axes of the slice: x: 4, y: 8, z: 8, core: 2. Of those that a mesh axis runs over, the one named last changes fastest.
Arguments:
- transfer: float32 [32768, 2048], P('row', 'col'), may hold values from -0.125 to 0.125
- emissions: float32 [2048, 4096], P('row', 'col'), may hold values from -6 to 6
Outputs:
- deposit: float32 [32768, 4096], P('row', 'col')
- checksum_rows: float32 [2, 4096], P(None, 'col')
- checksum_cols: float32 [2, 32768], P(None, 'row')
The draws below stay inside these ranges and needn't reach their ends.
All inputs are finite; a program needn't handle non-finite values.
Results may differ from the reference program's by a relative error of at most 0.00011.
Values sent between devices are 32-bit elements; how exact they have to be, the bound alone decides.
No kernel may reach another device: no remote copies, remote signals or barrier semaphores. Data moves between devices by JAX's collectives and lax.ppermute only.
A program may use at most 64 MiB of HBM per device.

```python
import jax
import jax.numpy as jnp
from jax import lax

K = 2048
M = 32768
S = 4096


def levels(stream_key, dims, cuts, least, largest):
    gain, own = 1.0, jax.random.fold_in(stream_key, 6)
    for position, shards_of in cuts:
        steps = jnp.exp(jax.random.uniform(jax.random.fold_in(own, position), (shards_of,), jnp.float32, least / len(cuts), largest / len(cuts)))
        gain = gain * jnp.repeat(steps, dims[position] // shards_of).reshape([-1 if axis == position else 1 for axis in range(len(dims))])
    return gain


def centred(own_key, extent, scale, most, pieces=(), kind=jnp.bfloat16):
    array = scale * jax.random.normal(own_key, extent, jnp.float32)
    if pieces:
        array = array * levels(own_key, extent, pieces, -0.22, 0.18)
    return jnp.clip(array, -most, most).astype(kind)


def setup_inputs(seed: int = 0) -> dict:
    key_list = jax.random.split(jax.random.key(seed), 3)
    transfer = centred(key_list[0], (M, K), K ** -0.5, 0.125, ((0, 32), (1, 16)), jnp.float32)
    emissions = centred(key_list[1], (K, S), 1.0, 6.0, ((0, 32), (1, 16)), jnp.float32)
    return {"transfer": transfer, "emissions": emissions}


def check_weights(total, start, count):
    index = (start + jnp.arange(count, dtype=jnp.int32)).astype(jnp.float32)
    flat = jnp.full((count,), 1.0, jnp.float32) / jnp.sqrt(jnp.float32(total))
    ramp = (index + 0.5) / total * jnp.sqrt(jnp.float32(3.0) / total)
    return jnp.stack([flat, ramp], 0)

def reference(transfer, emissions):
    deposit = jnp.dot(transfer, emissions, precision=lax.Precision.HIGHEST, preferred_element_type=jnp.float32)
    receptor_weights = check_weights(M, 0, M)
    scenario_weights = check_weights(S, 0, S)
    checksum_rows = jnp.dot(receptor_weights, deposit, precision=lax.Precision.HIGHEST, preferred_element_type=jnp.float32)
    checksum_cols = jnp.einsum('js,ms->jm', scenario_weights, deposit, precision=lax.Precision.HIGHEST, preferred_element_type=jnp.float32)
    return (deposit, checksum_rows, checksum_cols)
```

```python
import jax
import jax.numpy as jnp
from jax import lax
from jax.experimental import pallas as pl
from jax.experimental.pallas import tpu as pltpu
from jax.sharding import PartitionSpec as P

NX, NY, NZ = 4, 8, 8
STEP = 256
EXTRA = 8
VMEM = 48 * 1024 * 1024

Y_GROUPS = [[2 * y + c for y in range(NY)] for c in range(2)]
Z_GROUPS = [[NX * z + x for z in range(NZ)] for x in range(NX)]
SIBLING = [(j, j ^ 1) for j in range(2 * NY)]


def along_y(shift):
    return [(2 * y + c, 2 * ((y + shift) % NY) + c) for y in range(NY) for c in range(2)]


def spread(j):
    pairs = []
    for z in range(NZ):
        for x in range(NX):
            for y in range(NY):
                for c in range(2):
                    to = (2 * (x % 2) + c + j) % NX
                    pairs.append(((NX * z + x) * 2 * NY + 2 * y + c, (NX * z + to) * 2 * NY + 2 * y + x // 2))
    return pairs


def check_weights(total, start, count):
    index = (start + jnp.arange(count, dtype=jnp.int32)).astype(jnp.float32)
    flat = jnp.full((count,), 1.0, jnp.float32) / jnp.sqrt(jnp.float32(total))
    ramp = (index + 0.5) / total * jnp.sqrt(jnp.float32(3.0) / total)
    return jnp.stack([flat, ramp], 0)


def halves(value):
    high = value.astype(jnp.bfloat16)
    return high, (value - high.astype(jnp.float32)).astype(jnp.bfloat16)


def dot(left, right, contract=((1,), (0,))):
    return lax.dot_general(left, right, (contract, ((), ())), preferred_element_type=jnp.float32)


def product_kernel(place, *refs):
    blocks, (p4, m4, e, u, v, own, send, eh, el, vh, vl, sums) = refs[:7], refs[7:]
    y, c, i = place[0], place[1], pl.program_id(0)
    first = c == 0

    @pl.when(i == 0)
    def _():
        us = jnp.concatenate([u[k] for k in range(NY)], 1)
        sums[...] = lax.dot_general(
            us, e[...], (((1,), (0,)), ((), ())),
            precision=lax.Precision.HIGHEST, preferred_element_type=jnp.float32,
        )
        vs = []
        for k, shift in enumerate((0, -1, 1, -2, 2, -3, 3, 4)):
            at = lax.rem(y + shift + NY, NY)
            block = e[pl.ds(pl.multiple_of(at * 128, 128), 128), :]
            left, right = block[:, :256], block[:, 256:]
            block = jnp.concatenate([jnp.where(first, left, right), jnp.where(first, right, left)], 1)
            eh[k * 128 : (k + 1) * 128, :], el[k * 128 : (k + 1) * 128, :] = halves(block)
            vs.append(v[at])
        vh[...], vl[...] = halves(jnp.concatenate(vs, 1))

    last = jnp.where(i < 2, p4[...], m4[...])
    th, tl = halves(jnp.concatenate([b[...] for b in blocks] + [last], 1))
    out = dot(th, eh[...]) + (dot(tl, eh[...]) + dot(th, el[...]))
    lanes = ((1,), (1,))
    cols = dot(vh[...], th, lanes) + (dot(vl[...], th, lanes) + dot(vh[...], tl, lanes))
    own[:STEP, :] = out[:, :256]
    send[:STEP, :] = out[:, 256:]
    rows = sums[...]
    left, right = rows[:, :256], rows[:, 256:]
    zeros = jnp.zeros((EXTRA - 4, 256), jnp.float32)
    own[STEP:, :] = jnp.concatenate([cols, jnp.where(first, left, right), zeros], 0)
    send[STEP:, :] = jnp.concatenate([cols, jnp.where(first, right, left), zeros], 0)


def product(place, blocks, p4, m4, e, u, v):
    steps = blocks[0].shape[0] // STEP
    half = steps // 2
    whole = lambda a: pl.BlockSpec(a.shape, lambda i, s: (0,) * a.ndim)
    tall = STEP + EXTRA
    shape = jax.ShapeDtypeStruct((steps * tall, 256), jnp.float32)
    depth = e.shape[0]
    return pl.pallas_call(
        product_kernel,
        out_shape=(shape, shape),
        grid_spec=pltpu.PrefetchScalarGridSpec(
            num_scalar_prefetch=1,
            grid=(steps,),
            in_specs=[pl.BlockSpec((STEP, 128), lambda i, s: (i, 0))] * 7
            + [
                pl.BlockSpec((STEP, 128), lambda i, s: (jnp.minimum(i, half - 1), 0)),
                pl.BlockSpec((STEP, 128), lambda i, s: (jnp.maximum(i - half, 0), 0)),
                whole(e), whole(u), whole(v),
            ],
            out_specs=[pl.BlockSpec((tall, 256), lambda i, s: (i, 0))] * 2,
            scratch_shapes=[
                pltpu.VMEM((depth, 512), jnp.bfloat16),
                pltpu.VMEM((depth, 512), jnp.bfloat16),
                pltpu.VMEM((2, depth), jnp.bfloat16),
                pltpu.VMEM((2, depth), jnp.bfloat16),
                pltpu.VMEM((2, 512), jnp.float32),
            ],
        ),
        compiler_params=pltpu.CompilerParams(vmem_limit_bytes=VMEM),
    )(place, *blocks, p4, m4, e, u, v)


def join_kernel(own, other, main, rows, cols):
    total = own[...] + other[...]
    main[...] = total[:STEP]
    cols[...] = total[STEP : STEP + 2]
    rows[...] = total[STEP + 2 : STEP + 4]


def join(own, other):
    tall = STEP + EXTRA
    steps = own.shape[0] // tall
    return pl.pallas_call(
        join_kernel,
        out_shape=(
            jax.ShapeDtypeStruct((steps * STEP, 256), jnp.float32),
            jax.ShapeDtypeStruct((2, 256), jnp.float32),
            jax.ShapeDtypeStruct((2, steps * STEP), jnp.float32),
        ),
        grid=(steps,),
        in_specs=[pl.BlockSpec((tall, 256), lambda i: (i, 0))] * 2,
        out_specs=[
            pl.BlockSpec((STEP, 256), lambda i: (i, 0)),
            pl.BlockSpec((2, 256), lambda i: (0, 0)),
            pl.BlockSpec((2, STEP), lambda i: (0, i)),
        ],
    )(own, other)


def to_all(value, axis, count, groups=None):
    copies = jnp.broadcast_to(value[None], (count,) + value.shape)
    return lax.all_to_all(copies, axis, split_axis=0, concat_axis=0, axis_index_groups=groups)


def on_device(transfer, emissions):
    highest = lax.Precision.HIGHEST
    row, col = lax.axis_index("row"), lax.axis_index("col")
    x, y, c = lax.rem(row, NX), col // 2, lax.rem(col, 2)
    m_local = transfer.shape[0]
    up = lambda a: lax.ppermute(a, "col", along_y(1))
    down = lambda a: lax.ppermute(a, "col", along_y(-1))

    p1, m1 = up(transfer), down(transfer)
    p2, m2 = up(p1), down(m1)
    p3, m3 = up(p2), down(m2)
    p4, m4 = up(p3[: m_local // 2]), down(m3[m_local // 2 :])

    got = jnp.stack([lax.ppermute(emissions, ("row", "col"), spread(j)) for j in range(NX)])
    pick = [lax.dynamic_index_in_dim(got, lax.rem(x - s + NX, NX), keepdims=False) for s in range(NX)]
    near = jnp.concatenate(
        [jnp.concatenate(pick[:2], 1), jnp.concatenate(pick[2:], 1)], 0
    )
    whole = lax.all_gather(near, "row", axis=0, tiled=True, axis_index_groups=Z_GROUPS)

    receptor = check_weights(m_local * lax.axis_size("row"), row * m_local, m_local)
    u = jnp.dot(receptor, transfer, precision=highest, preferred_element_type=jnp.float32)
    u = to_all(u, "row", NX * NZ).sum(0)
    u = to_all(u, "col", NY, Y_GROUPS)

    scenario = check_weights(256 * lax.axis_size("col"), y * 512, 512)
    v = jnp.einsum("js,ks->jk", scenario, near, precision=highest, preferred_element_type=jnp.float32)
    v = to_all(v, "col", NY, Y_GROUPS).sum(0)
    v = to_all(v, "row", NZ, Z_GROUPS)

    place = jnp.stack([y, c]).astype(jnp.int32)
    own, send = product(place, [transfer, p1, m1, p2, m2, p3, m3], p4, m4, whole, u, v)
    other = lax.ppermute(send, "col", SIBLING)
    return join(own, other)


def solution(mesh):
    placed = (P("row", "col"), P("row", "col"))
    return jax.shard_map(
        on_device,
        mesh=mesh,
        in_specs=placed,
        out_specs=(P("row", "col"), P(None, "col"), P(None, "row")),
        check_vma=False,
    )
```

```python
import jax
import jax.numpy as jnp
from jax import lax
from jax.experimental import pallas as pl
from jax.experimental.pallas import tpu as pltpu
from jax.sharding import PartitionSpec as P

NX, NY, NZ = 4, 8, 8
STEP = 256
VMEM = 48 * 1024 * 1024

Z_GROUPS = [[NX * z + x for z in range(NZ)] for x in range(NX)]


def along_x(shift):
    return [(NX * z + x, NX * z + (x + shift) % NX) for z in range(NZ) for x in range(NX)]


def check_weights(total, start, count):
    index = (start + jnp.arange(count, dtype=jnp.int32)).astype(jnp.float32)
    flat = jnp.full((count,), 1.0, jnp.float32) / jnp.sqrt(jnp.float32(total))
    ramp = (index + 0.5) / total * jnp.sqrt(jnp.float32(3.0) / total)
    return jnp.stack([flat, ramp], 0)


def halves(value):
    high = value.astype(jnp.bfloat16)
    return high, (value - high.astype(jnp.float32)).astype(jnp.bfloat16)


def dot(left, right, contract=((1,), (0,))):
    return lax.dot_general(left, right, (contract, ((), ())), preferred_element_type=jnp.float32)


def three(left, right, contract=((1,), (0,))):
    (lh, ll), (rh, rl) = left, right
    return dot(lh, rh, contract) + (dot(ll, rh, contract) + dot(lh, rl, contract))


def product_kernel(place, t, e0, e1, e2, e3, u, v, main, rows, cols, eh, el):
    @pl.when(pl.program_id(0) == 0)
    def _():
        for d, part in enumerate((e0, e1, e2, e3)):
            x = lax.rem(place[0] + d, NX)
            for z in range(NZ):
                at = pl.ds(pl.multiple_of((NX * z + x) * 64, 64), 64)
                eh[at, :], el[at, :] = halves(part[z, :64, :])
        rows[...] = three(halves(u[...]), (eh[...], el[...]))

    th, tl = halves(jnp.concatenate([t[k] for k in range(t.shape[0])], 1))
    main[...] = three((th, tl), (eh[...], el[...]))
    cols[...] = three(halves(v[...]), (th, tl), ((1,), (1,)))


def product(place, t, parts, u, v):
    blocks, m, wide = t.shape
    whole = lambda a: pl.BlockSpec(a.shape, lambda i, s: (0,) * a.ndim)
    depth = blocks * wide
    return pl.pallas_call(
        product_kernel,
        out_shape=(
            jax.ShapeDtypeStruct((m, 256), jnp.float32),
            jax.ShapeDtypeStruct((2, 256), jnp.float32),
            jax.ShapeDtypeStruct((2, m), jnp.float32),
        ),
        grid_spec=pltpu.PrefetchScalarGridSpec(
            num_scalar_prefetch=1,
            grid=(m // STEP,),
            in_specs=[pl.BlockSpec((blocks, STEP, wide), lambda i, s: (0, i, 0))]
            + [whole(a) for a in (*parts, u, v)],
            out_specs=[
                pl.BlockSpec((STEP, 256), lambda i, s: (i, 0)),
                pl.BlockSpec((2, 256), lambda i, s: (0, 0)),
                pl.BlockSpec((2, STEP), lambda i, s: (0, i)),
            ],
            scratch_shapes=[pltpu.VMEM((depth, 256), jnp.bfloat16)] * 2,
        ),
        compiler_params=pltpu.CompilerParams(vmem_limit_bytes=VMEM),
    )(place, t, *parts, u, v)


def to_all(value, axis, count, groups=None):
    copies = jnp.broadcast_to(value[None], (count,) + value.shape)
    return lax.all_to_all(copies, axis, split_axis=0, concat_axis=0, axis_index_groups=groups)


def on_device(transfer, emissions):
    highest = lax.Precision.HIGHEST
    row, col = lax.axis_index("row"), lax.axis_index("col")
    x = lax.rem(row, NX)
    m_local, s_local = transfer.shape[0], emissions.shape[1]

    whole = lax.all_gather(transfer, "col", axis=0)

    receptor = check_weights(m_local * lax.axis_size("row"), row * m_local, m_local)
    u = jnp.dot(receptor, transfer, precision=highest, preferred_element_type=jnp.float32)
    sent = jnp.concatenate([emissions, jnp.pad(u, ((0, 6), (0, s_local - u.shape[1])))], 0)
    near = to_all(sent, "row", NZ, Z_GROUPS)
    parts = [near] + [lax.ppermute(near, "row", along_x(-d)) for d in (1, 2, 3)]
    u = sum(part[:, 64:66, :128].sum(0) for part in parts)
    u = to_all(u, "col", 2 * NY).transpose(1, 0, 2).reshape(2, -1)

    scenario = check_weights(s_local * lax.axis_size("col"), col * s_local, s_local)
    v = jnp.einsum("js,ks->jk", scenario, emissions, precision=highest, preferred_element_type=jnp.float32)
    v = to_all(v, "col", 2 * NY).sum(0)
    v = to_all(v, "row", NX * NZ).transpose(1, 0, 2).reshape(2, -1)

    place = jnp.stack([x]).astype(jnp.int32)
    return tuple(product(place, whole, parts, u, v))


def solution(mesh):
    placed = (P("row", "col"), P("row", "col"))
    return jax.shard_map(
        on_device,
        mesh=mesh,
        in_specs=placed,
        out_specs=(P("row", "col"), P(None, "col"), P(None, "row")),
        check_vma=False,
    )
```

```python
import jax
import jax.numpy as jnp
from jax import lax
from jax.experimental import pallas as pl
from jax.experimental.pallas import tpu as pltpu
from jax.sharding import PartitionSpec as P

NX, NY, NZ = 4, 8, 8
STEP = 256
PAD = 16
VMEM = 48 * 1024 * 1024
Z_ORDER = (0, 4, 2, 6, 1, 5, 3, 7)

RING = [(2 * y + c, 2 * ((y + 1 - 2 * c) % NY) + c) for y in range(NY) for c in range(2)]
SIBLING = [(j, j ^ 1) for j in range(2 * NY)]


def from_plane(dz, dx):
    return [
        (NX * ((z + dz) % NZ) + (x + dx) % NX, NX * z + x) for z in range(NZ) for x in range(NX)
    ]


def check_weights(total, start, count):
    index = (start + jnp.arange(count, dtype=jnp.int32)).astype(jnp.float32)
    flat = jnp.full((count,), 1.0, jnp.float32) / jnp.sqrt(jnp.float32(total))
    ramp = (index + 0.5) / total * jnp.sqrt(jnp.float32(3.0) / total)
    return jnp.stack([flat, ramp], 0)


def halves(value):
    high = value.astype(jnp.bfloat16)
    return high, (value - high.astype(jnp.float32)).astype(jnp.bfloat16)


def dot(left, right, contract=((1,), (0,))):
    return lax.dot_general(left, right, (contract, ((), ())), preferred_element_type=jnp.float32)


def product_kernel(place, *refs):
    blocks, (pair, four), parts, (u, v, main, rows, cols, eh, el, us, vs) = (
        refs[:10], refs[10:12], refs[12:16], refs[16:],
    )
    x, y, z, c = place[0], place[1], place[2], place[3]
    way = 2 * c - 1

    @pl.when(pl.program_id(0) == 0)
    def _():
        for d, part in enumerate(parts):
            from_x = lax.rem(x + d, NX)
            other = jnp.where(from_x // 2 == c, 0, 1)
            for i, dz in enumerate(Z_ORDER):
                away = lax.rem(way * (z + dz - y) + 4 * NY, NY)
                at = pl.multiple_of((2 * away + other) * 128 + lax.rem(from_x, 2) * 64, 64)
                eh[pl.ds(at, 64), :], el[pl.ds(at, 64), :] = halves(part[i * 64 : (i + 1) * 64, :])
        us[...] = jnp.zeros_like(us)
        for n in range(2 * NY):
            j = 2 * lax.rem(y + way * (n // 2) + NY, NY) + lax.rem(c + n, 2)
            us[:2, n * 128 : (n + 1) * 128] = u[j]
            vs[:, n * 128 : (n + 1) * 128] = v[j]

    t = [b[...] for b in blocks] + [pair[1], pair[0], four[3], four[2], four[1], four[0]]
    sums = []
    for w in range(2):
        total = t[0] * vs[w : w + 1, :128]
        for n in range(1, 2 * NY):
            total += t[n] * vs[w : w + 1, n * 128 : (n + 1) * 128]
        th, tl = halves(total)
        ones = jnp.ones((PAD, 128), jnp.bfloat16)
        lanes = ((1,), (1,))
        sums.append((dot(ones, th, lanes) + dot(ones, tl, lanes))[:1])
    cols[...] = jnp.concatenate(sums, 0)
    th, tl = halves(jnp.concatenate([jnp.concatenate(t, 1), us[...]], 0))
    out = dot(th, eh[...]) + (dot(tl, eh[...]) + dot(th, el[...]))
    main[...] = out[:STEP]
    rows[...] = out[STEP : STEP + 2]


def product(place, blocks, pair, four, parts, u, v):
    m, wide = blocks[0].shape
    whole = lambda a: pl.BlockSpec(a.shape, lambda i, s: (0,) * a.ndim)
    depth = 2 * NY * wide
    return pl.pallas_call(
        product_kernel,
        out_shape=(
            jax.ShapeDtypeStruct((m, 256), jnp.float32),
            jax.ShapeDtypeStruct((2, 256), jnp.float32),
            jax.ShapeDtypeStruct((2, m), jnp.float32),
        ),
        grid_spec=pltpu.PrefetchScalarGridSpec(
            num_scalar_prefetch=1,
            grid=(m // STEP,),
            in_specs=[pl.BlockSpec((STEP, wide), lambda i, s: (i, 0))] * 10
            + [pl.BlockSpec((a.shape[0], STEP, wide), lambda i, s: (0, i, 0)) for a in (pair, four)]
            + [whole(a) for a in (*parts, u, v)],
            out_specs=[
                pl.BlockSpec((STEP, 256), lambda i, s: (i, 0)),
                pl.BlockSpec((2, 256), lambda i, s: (0, 0)),
                pl.BlockSpec((2, STEP), lambda i, s: (0, i)),
            ],
            scratch_shapes=[pltpu.VMEM((depth, 256), jnp.bfloat16)] * 2
            + [pltpu.VMEM((PAD, depth), jnp.float32), pltpu.VMEM((2, depth), jnp.float32)],
        ),
        compiler_params=pltpu.CompilerParams(vmem_limit_bytes=VMEM),
    )(place, *blocks, pair, four, *parts, u, v)


def to_all(value, axis, count):
    copies = jnp.broadcast_to(value[None], (count,) + value.shape)
    return lax.all_to_all(copies, axis, split_axis=0, concat_axis=0)


def on_device(transfer, emissions):
    highest = lax.Precision.HIGHEST
    row, col = lax.axis_index("row"), lax.axis_index("col")
    x, z, y, c = lax.rem(row, NX), row // NX, col // 2, lax.rem(col, 2)
    m_local, s_local = transfer.shape[0], emissions.shape[1]
    pass_on = lambda a: lax.ppermute(a, "col", RING)
    swap = lambda a: lax.ppermute(a, "col", SIBLING)

    a1 = pass_on(transfer)
    s = swap(transfer)
    b1 = pass_on(s)

    receptor = check_weights(m_local * lax.axis_size("row"), row * m_local, m_local)
    u = jnp.dot(receptor, transfer, precision=highest, preferred_element_type=jnp.float32)
    scenario = check_weights(s_local * lax.axis_size("col"), col * s_local, s_local)
    v = jnp.einsum("js,ks->jk", scenario, emissions, precision=highest, preferred_element_type=jnp.float32)
    both = to_all(jnp.concatenate([u, v, jnp.zeros_like(v)], 1), "col", 2 * NY)
    v = both[:, :, 128:].sum(0)

    near = emissions
    for dz in (4, 2, 1):
        near = jnp.concatenate([near, lax.ppermute(near, "row", from_plane(dz, 0))], 0)
    parts = [near] + [lax.ppermute(near, "row", from_plane(0, d)) for d in (1, 2, 3)]

    both = to_all(jnp.concatenate([both[:, :, :128], v[None]], 0), "row", NX * NZ)
    u = both[:, : 2 * NY].sum(0)
    v = both[:, 2 * NY, :, :64].reshape(2 * NY, 2, 2, 64).transpose(0, 2, 1, 3).reshape(2 * NY, 2, 128)

    a2, b2 = pass_on(a1), pass_on(b1)
    a3, b3 = pass_on(a2), pass_on(b2)
    a4 = pass_on(a3)
    four = swap(jnp.stack([a1, b1, a2, b2]))
    pair = swap(jnp.stack([a3, b3]))
    b4 = swap(a4)
    place = jnp.stack([x, y, z, c]).astype(jnp.int32)
    return tuple(product(place, [transfer, s, a1, b1, a2, b2, a3, b3, a4, b4], pair, four, parts, u, v))


def solution(mesh):
    placed = (P("row", "col"), P("row", "col"))
    return jax.shard_map(
        on_device,
        mesh=mesh,
        in_specs=placed,
        out_specs=(P("row", "col"), P(None, "col"), P(None, "row")),
        check_vma=False,
    )
```

```python
import jax
import jax.numpy as jnp
from jax import lax
from jax.experimental import pallas as pl
from jax.experimental.pallas import tpu as pltpu
from jax.sharding import PartitionSpec as P

NX, NY, NZ = 4, 8, 8
STEP = 256
PAD = 16
VMEM = 48 * 1024 * 1024
Z_ORDER = (0, 4, 2, 6, 1, 5, 3, 7)


def from_plane(dz, dx):
    return [
        (NX * ((z + dz) % NZ) + (x + dx) % NX, NX * z + x) for z in range(NZ) for x in range(NX)
    ]


def check_weights(total, start, count):
    index = (start + jnp.arange(count, dtype=jnp.int32)).astype(jnp.float32)
    flat = jnp.full((count,), 1.0, jnp.float32) / jnp.sqrt(jnp.float32(total))
    ramp = (index + 0.5) / total * jnp.sqrt(jnp.float32(3.0) / total)
    return jnp.stack([flat, ramp], 0)


def halves(value):
    high = value.astype(jnp.bfloat16)
    return high, (value - high.astype(jnp.float32)).astype(jnp.bfloat16)


def dot(left, right, contract=((1,), (0,))):
    return lax.dot_general(left, right, (contract, ((), ())), preferred_element_type=jnp.float32)


def product_kernel(place, t, e0, e1, e2, e3, u, v, main, rows, cols, eh, el, us):
    @pl.when(pl.program_id(0) == 0)
    def _():
        for d, part in enumerate((e0, e1, e2, e3)):
            x = lax.rem(place[0] + d, NX)
            for i, dz in enumerate(Z_ORDER):
                z = lax.rem(place[1] + dz, NZ)
                at = pl.ds(pl.multiple_of((NX * z + x) * 64, 64), 64)
                eh[at, :], el[at, :] = halves(part[i * 64 : (i + 1) * 64, :])
        us[...] = jnp.zeros_like(us)
        for n in range(2 * NY):
            us[:2, n * 128 : (n + 1) * 128] = u[n]

    blocks = [t[n] for n in range(2 * NY)]
    sums = []
    for w in range(2):
        total = blocks[0] * v[0, w : w + 1, :]
        for n in range(1, 2 * NY):
            total += blocks[n] * v[n, w : w + 1, :]
        th, tl = halves(total)
        ones = jnp.ones((PAD, 128), jnp.bfloat16)
        lanes = ((1,), (1,))
        sums.append((dot(ones, th, lanes) + dot(ones, tl, lanes))[:1])
    cols[...] = jnp.concatenate(sums, 0)
    th, tl = halves(jnp.concatenate([jnp.concatenate(blocks, 1), us[...]], 0))
    out = dot(th, eh[...]) + (dot(tl, eh[...]) + dot(th, el[...]))
    main[...] = out[:STEP]
    rows[...] = out[STEP : STEP + 2]


def product(place, t, parts, u, v):
    blocks, m, wide = t.shape
    whole = lambda a: pl.BlockSpec(a.shape, lambda i, s: (0,) * a.ndim)
    depth = blocks * wide
    return pl.pallas_call(
        product_kernel,
        out_shape=(
            jax.ShapeDtypeStruct((m, 256), jnp.float32),
            jax.ShapeDtypeStruct((2, 256), jnp.float32),
            jax.ShapeDtypeStruct((2, m), jnp.float32),
        ),
        grid_spec=pltpu.PrefetchScalarGridSpec(
            num_scalar_prefetch=1,
            grid=(m // STEP,),
            in_specs=[pl.BlockSpec((blocks, STEP, wide), lambda i, s: (0, i, 0))]
            + [whole(a) for a in (*parts, u, v)],
            out_specs=[
                pl.BlockSpec((STEP, 256), lambda i, s: (i, 0)),
                pl.BlockSpec((2, 256), lambda i, s: (0, 0)),
                pl.BlockSpec((2, STEP), lambda i, s: (0, i)),
            ],
            scratch_shapes=[pltpu.VMEM((depth, 256), jnp.bfloat16)] * 2
            + [pltpu.VMEM((PAD, depth), jnp.float32)],
        ),
        compiler_params=pltpu.CompilerParams(vmem_limit_bytes=VMEM),
    )(place, t, *parts, u, v)


def to_all(value, axis, count):
    copies = jnp.broadcast_to(value[None], (count,) + value.shape)
    return lax.all_to_all(copies, axis, split_axis=0, concat_axis=0)


def on_device(transfer, emissions):
    highest = lax.Precision.HIGHEST
    row, col = lax.axis_index("row"), lax.axis_index("col")
    x, z = lax.rem(row, NX), row // NX
    m_local, s_local = transfer.shape[0], emissions.shape[1]
    whole = lax.all_gather(transfer, "col", axis=0)

    receptor = check_weights(m_local * lax.axis_size("row"), row * m_local, m_local)
    u = jnp.dot(receptor, transfer, precision=highest, preferred_element_type=jnp.float32)
    scenario = check_weights(s_local * lax.axis_size("col"), col * s_local, s_local)
    v = jnp.einsum("js,ks->jk", scenario, emissions, precision=highest, preferred_element_type=jnp.float32)
    both = to_all(jnp.concatenate([u, v, jnp.zeros_like(v)], 1), "col", 2 * NY)
    v = both[:, :, 128:].sum(0)

    near = emissions
    for dz in (4, 2, 1):
        near = jnp.concatenate([near, lax.ppermute(near, "row", from_plane(dz, 0))], 0)
    parts = [near] + [lax.ppermute(near, "row", from_plane(0, d)) for d in (1, 2, 3)]

    both = to_all(jnp.concatenate([both[:, :, :128], v[None]], 0), "row", NX * NZ)
    u = both[:, : 2 * NY].sum(0)
    v = both[:, 2 * NY, :, :64].reshape(2 * NY, 2, 2, 64).transpose(0, 2, 1, 3).reshape(2 * NY, 2, 128)

    place = jnp.stack([x, z]).astype(jnp.int32)
    return tuple(product(place, whole, parts, u, v))


def solution(mesh):
    placed = (P("row", "col"), P("row", "col"))
    return jax.shard_map(
        on_device,
        mesh=mesh,
        in_specs=placed,
        out_specs=(P("row", "col"), P(None, "col"), P(None, "row")),
        check_vma=False,
    )
```

```python
import jax
import jax.numpy as jnp
from jax import lax
from jax.experimental import pallas as pl
from jax.experimental.pallas import tpu as pltpu
from jax.sharding import PartitionSpec as P

NX, NY, NZ = 4, 8, 8
STEP = 256
PAD = 16
VMEM = 48 * 1024 * 1024
DEPTH = 64 * NZ

Z_GROUPS = [[NX * z + x for z in range(NZ)] for x in range(NX)]


def from_x(dx):
    return [(NX * z + (x + dx) % NX, NX * z + x) for z in range(NZ) for x in range(NX)]


def check_weights(total, start, count):
    index = (start + jnp.arange(count, dtype=jnp.int32)).astype(jnp.float32)
    flat = jnp.full((count,), 1.0, jnp.float32) / jnp.sqrt(jnp.float32(total))
    ramp = (index + 0.5) / total * jnp.sqrt(jnp.float32(3.0) / total)
    return jnp.stack([flat, ramp], 0)


def halves(value):
    high = value.astype(jnp.bfloat16)
    return high, (value - high.astype(jnp.float32)).astype(jnp.bfloat16)


def dot(left, right, contract=((1,), (0,))):
    return lax.dot_general(left, right, (contract, ((), ())), preferred_element_type=jnp.float32)


def product_kernel(place, t, e0, e1, e2, e3, main, rows, cols, eh, el, us, v):
    @pl.when(pl.program_id(0) == 0)
    def _():
        v[...] = jnp.zeros_like(v)
        upper = lax.broadcasted_iota(jnp.int32, (1, 128), 1) // 64
        for d, part in enumerate((e0, e1, e2, e3)):
            x = lax.rem(place[0] + d, NX)
            here = upper == lax.rem(x, 2)
            for z in range(NZ):
                at = pl.ds(pl.multiple_of((NX * z + x) * 64, 64), 64)
                eh[at, :], el[at, :] = halves(part[z * 64 : (z + 1) * 64, :])
                own = part[DEPTH + 16 + z : DEPTH + 17 + z, :]
                both = jnp.concatenate([own[:, :128], own[:, 128:]], 0)
                v[2 * z + x // 2] += jnp.where(here, both, 0.0)
        us[...] = jnp.zeros_like(us)
        total = (e0[DEPTH : DEPTH + 16, :] + e1[DEPTH : DEPTH + 16, :]) + (
            e2[DEPTH : DEPTH + 16, :] + e3[DEPTH : DEPTH + 16, :]
        )
        for n in range(2 * NY):
            for w in range(2):
                us[w : w + 1, n * 128 : (n + 1) * 128] = total[n : n + 1, w * 128 : (w + 1) * 128]

    blocks = [t[n] for n in range(2 * NY)]
    sums = []
    for w in range(2):
        total = blocks[0] * v[0, w : w + 1, :]
        for n in range(1, 2 * NY):
            total += blocks[n] * v[n, w : w + 1, :]
        th, tl = halves(total)
        ones = jnp.ones((PAD, 128), jnp.bfloat16)
        lanes = ((1,), (1,))
        sums.append((dot(ones, th, lanes) + dot(ones, tl, lanes))[:1])
    cols[...] = jnp.concatenate(sums, 0)
    th, tl = halves(jnp.concatenate([jnp.concatenate(blocks, 1), us[...]], 0))
    out = dot(th, eh[...]) + (dot(tl, eh[...]) + dot(th, el[...]))
    main[...] = out[:STEP]
    rows[...] = out[STEP : STEP + 2]


def product(place, t, parts):
    blocks, m, wide = t.shape
    whole = lambda a: pl.BlockSpec(a.shape, lambda i, s: (0,) * a.ndim)
    depth = blocks * wide
    return pl.pallas_call(
        product_kernel,
        out_shape=(
            jax.ShapeDtypeStruct((m, 256), jnp.float32),
            jax.ShapeDtypeStruct((2, 256), jnp.float32),
            jax.ShapeDtypeStruct((2, m), jnp.float32),
        ),
        grid_spec=pltpu.PrefetchScalarGridSpec(
            num_scalar_prefetch=1,
            grid=(m // STEP,),
            in_specs=[pl.BlockSpec((blocks, STEP, wide), lambda i, s: (0, i, 0))]
            + [whole(a) for a in parts],
            out_specs=[
                pl.BlockSpec((STEP, 256), lambda i, s: (i, 0)),
                pl.BlockSpec((2, 256), lambda i, s: (0, 0)),
                pl.BlockSpec((2, STEP), lambda i, s: (0, i)),
            ],
            scratch_shapes=[pltpu.VMEM((depth, 256), jnp.bfloat16)] * 2
            + [pltpu.VMEM((PAD, depth), jnp.float32), pltpu.VMEM((blocks, 2, wide), jnp.float32)],
        ),
        compiler_params=pltpu.CompilerParams(vmem_limit_bytes=VMEM),
    )(place, t, *parts)


def to_all(value, axis, count, groups=None):
    copies = jnp.broadcast_to(value[None], (count,) + value.shape)
    return lax.all_to_all(copies, axis, split_axis=0, concat_axis=0, axis_index_groups=groups)


def on_device(transfer, emissions):
    highest = lax.Precision.HIGHEST
    row, col = lax.axis_index("row"), lax.axis_index("col")
    x = lax.rem(row, NX)
    m_local, s_local = transfer.shape[0], emissions.shape[1]
    whole = lax.all_gather(transfer, "col", axis=0)

    receptor = check_weights(m_local * lax.axis_size("row"), row * m_local, m_local)
    u = jnp.dot(receptor, transfer, precision=highest, preferred_element_type=jnp.float32)
    scenario = check_weights(s_local * lax.axis_size("col"), col * s_local, s_local)
    v = jnp.einsum("js,ks->jk", scenario, emissions, precision=highest, preferred_element_type=jnp.float32)
    both = to_all(jnp.concatenate([u, v, jnp.zeros_like(v)], 1), "col", 2 * NY)
    v = both[:, :, 128:192].sum(0)
    v = jnp.concatenate([v[:1], v[:1], v[1:], v[1:]], 1)
    sent = jnp.concatenate(
        [emissions, both[:, :, :128].reshape(2 * NY, s_local), v, jnp.zeros((7, s_local), jnp.float32)], 0
    )

    near = to_all(sent, "row", NZ, Z_GROUPS)
    near = jnp.concatenate([near[:, :64].reshape(DEPTH, s_local), near[:, 64:80].sum(0), near[:, 80]], 0)
    parts = [near] + [lax.ppermute(near, "row", from_x(d)) for d in (1, 2, 3)]

    place = jnp.stack([x]).astype(jnp.int32)
    return tuple(product(place, whole, parts))


def solution(mesh):
    placed = (P("row", "col"), P("row", "col"))
    return jax.shard_map(
        on_device,
        mesh=mesh,
        in_specs=placed,
        out_specs=(P("row", "col"), P(None, "col"), P(None, "row")),
        check_vma=False,
    )
```

```python
import jax
import jax.numpy as jnp
from jax import lax
from jax.experimental import pallas as pl
from jax.experimental.pallas import tpu as pltpu
from jax.sharding import PartitionSpec as P

NX, NY, NZ = 4, 8, 8
STEP = 256
PAD = 16
VMEM = 40 * 1024 * 1024
DEPTH = 64 * NZ

Z_GROUPS = [[NX * z + x for z in range(NZ)] for x in range(NX)]


def from_x(dx):
    return [(NX * z + (x + dx) % NX, NX * z + x) for z in range(NZ) for x in range(NX)]


def check_weights(total, start, count):
    index = (start + jnp.arange(count, dtype=jnp.int32)).astype(jnp.float32)
    flat = jnp.full((count,), 1.0, jnp.float32) / jnp.sqrt(jnp.float32(total))
    ramp = (index + 0.5) / total * jnp.sqrt(jnp.float32(3.0) / total)
    return jnp.stack([flat, ramp], 0)


def halves(value):
    high = value.astype(jnp.bfloat16)
    return high, (value - high.astype(jnp.float32)).astype(jnp.bfloat16)


def dot(left, right, contract=((1,), (0,))):
    return lax.dot_general(left, right, (contract, ((), ())), preferred_element_type=jnp.float32)


def split_kernel(t, high, low):
    high[...], low[...] = halves(jnp.concatenate([t[n] for n in range(t.shape[0])], 1))


def split(t):
    blocks, m, wide = t.shape
    shape = jax.ShapeDtypeStruct((m, blocks * wide), jnp.bfloat16)
    return pl.pallas_call(
        split_kernel,
        out_shape=(shape, shape),
        grid=(m // STEP,),
        in_specs=[pl.BlockSpec((blocks, STEP, wide), lambda i: (0, i, 0))],
        out_specs=[pl.BlockSpec((STEP, blocks * wide), lambda i: (i, 0))] * 2,
        compiler_params=pltpu.CompilerParams(vmem_limit_bytes=VMEM),
    )(t)


def product_kernel(place, th, tl, e0, e1, e2, e3, main, rows, cols, mv, eh, el, v, gone):
    v[...] = jnp.zeros_like(v)
    upper = lax.broadcasted_iota(jnp.int32, (1, 128), 1) // 64
    for d, part in enumerate((e0, e1, e2, e3)):
        x = lax.rem(place[0] + d, NX)
        here = upper == lax.rem(x, 2)
        for z in range(NZ):
            at = pl.ds(pl.multiple_of((NX * z + x) * 64, 64), 64)
            eh[at, :], el[at, :] = halves(part[z * 64 : (z + 1) * 64, :])
            own = part[DEPTH + 16 + z : DEPTH + 17 + z, :]
            both = jnp.concatenate([own[:, :128], own[:, 128:]], 0)
            v[2 * z + x // 2] += jnp.where(here, both, 0.0)
    total = (e0[DEPTH : DEPTH + 16, :] + e1[DEPTH : DEPTH + 16, :]) + (
        e2[DEPTH : DEPTH + 16, :] + e3[DEPTH : DEPTH + 16, :]
    )
    us = [jnp.concatenate([total[n : n + 1, w : w + 128] for n in range(2 * NY)], 1) for w in (0, 128)]
    uh, ul = halves(jnp.concatenate(us + [jnp.zeros((PAD - 2, us[0].shape[1]), jnp.float32)], 0))
    ones = jnp.ones((PAD, 128), jnp.bfloat16)
    lanes = ((1,), (1,))

    stores = []
    for i in range(mv.shape[0]):
        at = slice(i * STEP, (i + 1) * STEP)
        left, right = th[at, :], tl[at, :]
        if i == 0:
            left, right = jnp.concatenate([left, uh], 0), jnp.concatenate([right, ul], 0)
        out = dot(left, eh[...]) + (dot(right, eh[...]) + dot(left, el[...]))
        mv[i] = out[:STEP]
        if i == 0:
            rows[...] = out[STEP : STEP + 2]
        stores.append(pltpu.make_async_copy(mv.at[i], main.at[pl.ds(i * STEP, STEP), :], gone.at[i]))
        stores[i].start()
        sums = [0.0, 0.0]
        for n in range(2 * NY):
            k = slice(n * 128, (n + 1) * 128)
            block = th[at, k].astype(jnp.float32) + tl[at, k].astype(jnp.float32)
            for w in range(2):
                sums[w] += block * v[n, w : w + 1, :]
        for w in range(2):
            sh, sl = halves(sums[w])
            cols[w : w + 1, at] = (dot(ones, sh, lanes) + dot(ones, sl, lanes))[:1]
    for store in stores:
        store.wait()


def product(place, th, tl, parts):
    m, depth = th.shape
    steps = m // STEP
    vmem = pl.BlockSpec(memory_space=pltpu.VMEM)
    return pl.pallas_call(
        product_kernel,
        out_shape=(
            jax.ShapeDtypeStruct((m, 256), jnp.float32),
            jax.ShapeDtypeStruct((2, 256), jnp.float32),
            jax.ShapeDtypeStruct((2, m), jnp.float32),
        ),
        in_specs=[pl.BlockSpec(memory_space=pltpu.SMEM)] + [vmem] * 6,
        out_specs=[pl.BlockSpec(memory_space=pl.ANY), vmem, vmem],
        scratch_shapes=[
            pltpu.VMEM((steps, STEP, 256), jnp.float32),
            pltpu.VMEM((depth, 256), jnp.bfloat16),
            pltpu.VMEM((depth, 256), jnp.bfloat16),
            pltpu.VMEM((2 * NY, 2, 128), jnp.float32),
            pltpu.SemaphoreType.DMA((steps,)),
        ],
        compiler_params=pltpu.CompilerParams(vmem_limit_bytes=VMEM),
    )(place, th, tl, *parts)


def to_all(value, axis, count, groups=None):
    copies = jnp.broadcast_to(value[None], (count,) + value.shape)
    return lax.all_to_all(copies, axis, split_axis=0, concat_axis=0, axis_index_groups=groups)


def on_device(transfer, emissions):
    highest = lax.Precision.HIGHEST
    row, col = lax.axis_index("row"), lax.axis_index("col")
    x = lax.rem(row, NX)
    m_local, s_local = transfer.shape[0], emissions.shape[1]
    whole = lax.all_gather(transfer, "col", axis=0)

    receptor = check_weights(m_local * lax.axis_size("row"), row * m_local, m_local)
    u = jnp.dot(receptor, transfer, precision=highest, preferred_element_type=jnp.float32)
    scenario = check_weights(s_local * lax.axis_size("col"), col * s_local, s_local)
    v = jnp.einsum("js,ks->jk", scenario, emissions, precision=highest, preferred_element_type=jnp.float32)
    both = to_all(jnp.concatenate([u, v, jnp.zeros_like(v)], 1), "col", 2 * NY)
    v = both[:, :, 128:192].sum(0)
    v = jnp.concatenate([v[:1], v[:1], v[1:], v[1:]], 1)
    sent = jnp.concatenate(
        [emissions, both[:, :, :128].reshape(2 * NY, s_local), v, jnp.zeros((7, s_local), jnp.float32)], 0
    )

    near = to_all(sent, "row", NZ, Z_GROUPS)
    near = jnp.concatenate([near[:, :64].reshape(DEPTH, s_local), near[:, 64:80].sum(0), near[:, 80]], 0)
    parts = [near] + [lax.ppermute(near, "row", from_x(d)) for d in (1, 2, 3)]

    place = jnp.stack([x]).astype(jnp.int32)
    return tuple(product(place, *split(whole), parts))


def solution(mesh):
    placed = (P("row", "col"), P("row", "col"))
    return jax.shard_map(
        on_device,
        mesh=mesh,
        in_specs=placed,
        out_specs=(P("row", "col"), P(None, "col"), P(None, "row")),
        check_vma=False,
    )
```

```python
import jax
import jax.numpy as jnp
from jax import lax
from jax.experimental import pallas as pl
from jax.experimental.pallas import tpu as pltpu
from jax.sharding import PartitionSpec as P

NX, NY, NZ = 4, 8, 8
STEP = 256
PAD = 16
VMEM = 48 * 1024 * 1024

Z_GROUPS = [[NX * z + x for z in range(NZ)] for x in range(NX)]


def from_x(dx):
    return [(NX * z + (x + dx) % NX, NX * z + x) for z in range(NZ) for x in range(NX)]


def check_weights(total, start, count):
    index = (start + jnp.arange(count, dtype=jnp.int32)).astype(jnp.float32)
    flat = jnp.full((count,), 1.0, jnp.float32) / jnp.sqrt(jnp.float32(total))
    ramp = (index + 0.5) / total * jnp.sqrt(jnp.float32(3.0) / total)
    return jnp.stack([flat, ramp], 0)


def halves(value):
    high = value.astype(jnp.bfloat16)
    return high, (value - high.astype(jnp.float32)).astype(jnp.bfloat16)


def dot(left, right, contract=((1,), (0,))):
    return lax.dot_general(left, right, (contract, ((), ())), preferred_element_type=jnp.float32)


def product_kernel(place, t, e0, e1, e2, e3, both, main, rows, cols, eh, el, us, v):
    @pl.when(pl.program_id(0) == 0)
    def _():
        for d, part in enumerate((e0, e1, e2, e3)):
            x = lax.rem(place[0] + d, NX)
            for z in range(NZ):
                at = pl.ds(pl.multiple_of((NX * z + x) * 64, 64), 64)
                eh[at, :], el[at, :] = halves(part[z])
        us[...] = jnp.zeros_like(us)
        u = both[0, : 2 * NY]
        for r in range(1, NX * NZ):
            u += both[r, : 2 * NY]
        for n in range(2 * NY):
            us[:2, n * 128 : (n + 1) * 128] = u[n]
            v[n] = jnp.concatenate([both[2 * n + k, 2 * NY, :, :64] for k in range(2)], 1)

    blocks = [t[n] for n in range(2 * NY)]
    sums = []
    for w in range(2):
        total = blocks[0] * v[0, w : w + 1, :]
        for n in range(1, 2 * NY):
            total += blocks[n] * v[n, w : w + 1, :]
        th, tl = halves(total)
        ones = jnp.ones((PAD, 128), jnp.bfloat16)
        lanes = ((1,), (1,))
        sums.append((dot(ones, th, lanes) + dot(ones, tl, lanes))[:1])
    cols[...] = jnp.concatenate(sums, 0)
    th, tl = halves(jnp.concatenate([jnp.concatenate(blocks, 1), us[...]], 0))
    out = dot(th, eh[...]) + (dot(tl, eh[...]) + dot(th, el[...]))
    main[...] = out[:STEP]
    rows[...] = out[STEP : STEP + 2]


def product(place, t, parts, both):
    blocks, m, wide = t.shape
    whole = lambda a: pl.BlockSpec(a.shape, lambda i, s: (0,) * a.ndim)
    depth = blocks * wide
    return pl.pallas_call(
        product_kernel,
        out_shape=(
            jax.ShapeDtypeStruct((m, 256), jnp.float32),
            jax.ShapeDtypeStruct((2, 256), jnp.float32),
            jax.ShapeDtypeStruct((2, m), jnp.float32),
        ),
        grid_spec=pltpu.PrefetchScalarGridSpec(
            num_scalar_prefetch=1,
            grid=(m // STEP,),
            in_specs=[pl.BlockSpec((blocks, STEP, wide), lambda i, s: (0, i, 0))]
            + [whole(a) for a in (*parts, both)],
            out_specs=[
                pl.BlockSpec((STEP, 256), lambda i, s: (i, 0)),
                pl.BlockSpec((2, 256), lambda i, s: (0, 0)),
                pl.BlockSpec((2, STEP), lambda i, s: (0, i)),
            ],
            scratch_shapes=[pltpu.VMEM((depth, 256), jnp.bfloat16)] * 2
            + [pltpu.VMEM((PAD, depth), jnp.float32), pltpu.VMEM((blocks, 2, wide), jnp.float32)],
        ),
        compiler_params=pltpu.CompilerParams(vmem_limit_bytes=VMEM),
    )(place, t, *parts, both)


def to_all(value, axis, count, groups=None):
    copies = jnp.broadcast_to(value[None], (count,) + value.shape)
    return lax.all_to_all(copies, axis, split_axis=0, concat_axis=0, axis_index_groups=groups)


def on_device(transfer, emissions):
    highest = lax.Precision.HIGHEST
    row, col = lax.axis_index("row"), lax.axis_index("col")
    x = lax.rem(row, NX)
    m_local, s_local = transfer.shape[0], emissions.shape[1]
    whole = lax.all_gather(transfer, "col", axis=0)

    near = to_all(emissions, "row", NZ, Z_GROUPS)
    parts = [near] + [lax.ppermute(near, "row", from_x(d)) for d in (1, 2, 3)]

    receptor = check_weights(m_local * lax.axis_size("row"), row * m_local, m_local)
    u = jnp.dot(receptor, transfer, precision=highest, preferred_element_type=jnp.float32)
    scenario = check_weights(s_local * lax.axis_size("col"), col * s_local, s_local)
    v = jnp.einsum("js,ks->jk", scenario, emissions, precision=highest, preferred_element_type=jnp.float32)
    small = jnp.concatenate([u, v, jnp.zeros_like(v)], 1)
    small, near = lax.optimization_barrier((small, near))
    both = to_all(small, "col", 2 * NY)
    both = jnp.concatenate([both[:, :, :128], both[:, :, 128:].sum(0)[None]], 0)
    both, parts[1], parts[3] = lax.optimization_barrier((both, parts[1], parts[3]))
    both = to_all(both, "row", NX * NZ)

    place = jnp.stack([x]).astype(jnp.int32)
    return tuple(product(place, whole, parts, both))


def solution(mesh):
    placed = (P("row", "col"), P("row", "col"))
    return jax.shard_map(
        on_device,
        mesh=mesh,
        in_specs=placed,
        out_specs=(P("row", "col"), P(None, "col"), P(None, "row")),
        check_vma=False,
    )
```

```python
import jax
import jax.numpy as jnp
from jax import lax
from jax.experimental import pallas as pl
from jax.experimental.pallas import tpu as pltpu
from jax.sharding import PartitionSpec as P

NX, NY, NZ = 4, 8, 8
STEP = 256
PAD = 16
VMEM = 48 * 1024 * 1024

Z_GROUPS = [[NX * z + x for z in range(NZ)] for x in range(NX)]


def from_x(dx):
    return [(NX * z + (x + dx) % NX, NX * z + x) for z in range(NZ) for x in range(NX)]


def check_weights(total, start, count):
    index = (start + jnp.arange(count, dtype=jnp.int32)).astype(jnp.float32)
    flat = jnp.full((count,), 1.0, jnp.float32) / jnp.sqrt(jnp.float32(total))
    ramp = (index + 0.5) / total * jnp.sqrt(jnp.float32(3.0) / total)
    return jnp.stack([flat, ramp], 0)


def halves(value):
    high = value.astype(jnp.bfloat16)
    return high, (value - high.astype(jnp.float32)).astype(jnp.bfloat16)


def dot(left, right, contract=((1,), (0,))):
    return lax.dot_general(left, right, (contract, ((), ())), preferred_element_type=jnp.float32)


def product_kernel(place, t, e0, e1, e2, e2_more, e3, both, main, rows, cols, eh, el, us, v):
    @pl.when(pl.program_id(0) == 0)
    def _():
        for d, part in enumerate(((e0,), (e1,), (e2, e2_more), (e3,))):
            x = lax.rem(place[0] + d, NX)
            for z in range(NZ):
                at = pl.ds(pl.multiple_of((NX * z + x) * 64, 64), 64)
                eh[at, :], el[at, :] = halves(part[z * len(part) // NZ][z % (NZ // len(part))])
        us[...] = jnp.zeros_like(us)
        u = both[0, : 2 * NY]
        for r in range(1, NX * NZ):
            u += both[r, : 2 * NY]
        for n in range(2 * NY):
            us[:2, n * 128 : (n + 1) * 128] = u[n]
            v[n] = jnp.concatenate([both[2 * n + k, 2 * NY, :, :64] for k in range(2)], 1)

    blocks = [t[n] for n in range(2 * NY)]
    sums = []
    for w in range(2):
        total = blocks[0] * v[0, w : w + 1, :]
        for n in range(1, 2 * NY):
            total += blocks[n] * v[n, w : w + 1, :]
        th, tl = halves(total)
        ones = jnp.ones((PAD, 128), jnp.bfloat16)
        lanes = ((1,), (1,))
        sums.append((dot(ones, th, lanes) + dot(ones, tl, lanes))[:1])
    cols[...] = jnp.concatenate(sums, 0)
    th, tl = halves(jnp.concatenate([jnp.concatenate(blocks, 1), us[...]], 0))
    out = dot(th, eh[...]) + (dot(tl, eh[...]) + dot(th, el[...]))
    main[...] = out[:STEP]
    rows[...] = out[STEP : STEP + 2]


def product(place, t, parts, both):
    blocks, m, wide = t.shape
    whole = lambda a: pl.BlockSpec(a.shape, lambda i, s: (0,) * a.ndim)
    depth = blocks * wide
    return pl.pallas_call(
        product_kernel,
        out_shape=(
            jax.ShapeDtypeStruct((m, 256), jnp.float32),
            jax.ShapeDtypeStruct((2, 256), jnp.float32),
            jax.ShapeDtypeStruct((2, m), jnp.float32),
        ),
        grid_spec=pltpu.PrefetchScalarGridSpec(
            num_scalar_prefetch=1,
            grid=(m // STEP,),
            in_specs=[pl.BlockSpec((blocks, STEP, wide), lambda i, s: (0, i, 0))]
            + [whole(a) for a in (*parts, both)],
            out_specs=[
                pl.BlockSpec((STEP, 256), lambda i, s: (i, 0)),
                pl.BlockSpec((2, 256), lambda i, s: (0, 0)),
                pl.BlockSpec((2, STEP), lambda i, s: (0, i)),
            ],
            scratch_shapes=[pltpu.VMEM((depth, 256), jnp.bfloat16)] * 2
            + [pltpu.VMEM((PAD, depth), jnp.float32), pltpu.VMEM((blocks, 2, wide), jnp.float32)],
        ),
        compiler_params=pltpu.CompilerParams(vmem_limit_bytes=VMEM),
    )(place, t, *parts, both)


def to_all(value, axis, count, groups=None):
    copies = jnp.broadcast_to(value[None], (count,) + value.shape)
    return lax.all_to_all(copies, axis, split_axis=0, concat_axis=0, axis_index_groups=groups)


def on_device(transfer, emissions):
    highest = lax.Precision.HIGHEST
    row, col = lax.axis_index("row"), lax.axis_index("col")
    x = lax.rem(row, NX)
    m_local, s_local = transfer.shape[0], emissions.shape[1]
    whole = lax.all_gather(transfer, "col", axis=0)

    near = to_all(emissions, "row", NZ, Z_GROUPS)
    after, before = [lax.ppermute(near, "row", from_x(d)) for d in (1, 3)]

    receptor = check_weights(m_local * lax.axis_size("row"), row * m_local, m_local)
    u = jnp.dot(receptor, transfer, precision=highest, preferred_element_type=jnp.float32)
    scenario = check_weights(s_local * lax.axis_size("col"), col * s_local, s_local)
    v = jnp.einsum("js,ks->jk", scenario, emissions, precision=highest, preferred_element_type=jnp.float32)
    small = jnp.concatenate([u, v, jnp.zeros_like(v)], 1)
    small, near = lax.optimization_barrier((small, near))
    both = to_all(small, "col", 2 * NY)
    both = jnp.concatenate([both[:, :, :128], both[:, :, 128:].sum(0)[None]], 0)
    both, after, before = lax.optimization_barrier((both, after, before))
    both = to_all(both, "row", NX * NZ)

    two = [
        lax.ppermute(after[: NZ // 2], "row", from_x(1)),
        lax.ppermute(before[NZ // 2 :], "row", from_x(3)),
    ]
    parts = [near, after, *two, before]

    place = jnp.stack([x]).astype(jnp.int32)
    return tuple(product(place, whole, parts, both))


def solution(mesh):
    placed = (P("row", "col"), P("row", "col"))
    return jax.shard_map(
        on_device,
        mesh=mesh,
        in_specs=placed,
        out_specs=(P("row", "col"), P(None, "col"), P(None, "row")),
        check_vma=False,
    )
```

```python
import jax
import jax.numpy as jnp
from jax import lax
from jax.experimental import pallas as pl
from jax.experimental.pallas import tpu as pltpu
from jax.sharding import PartitionSpec as P

NX, NY, NZ = 4, 8, 8
STEP = 256
PAD = 16
VMEM = 48 * 1024 * 1024

Z_GROUPS = [[NX * z + x for z in range(NZ)] for x in range(NX)]


def from_x(dx):
    return [(NX * z + (x + dx) % NX, NX * z + x) for z in range(NZ) for x in range(NX)]


def check_weights(total, start, count):
    index = (start + jnp.arange(count, dtype=jnp.int32)).astype(jnp.float32)
    flat = jnp.full((count,), 1.0, jnp.float32) / jnp.sqrt(jnp.float32(total))
    ramp = (index + 0.5) / total * jnp.sqrt(jnp.float32(3.0) / total)
    return jnp.stack([flat, ramp], 0)


def halves(value):
    high = value.astype(jnp.bfloat16)
    return high, (value - high.astype(jnp.float32)).astype(jnp.bfloat16)


def dot(left, right, contract=((1,), (0,))):
    return lax.dot_general(left, right, (contract, ((), ())), preferred_element_type=jnp.float32)


def product_kernel(place, t, e0, e1, e2, e2_more, e3, both, main, rows, cols, eh, el, us, v):
    @pl.when(pl.program_id(0) == 0)
    def _():
        for d, part in enumerate(((e0,), (e1,), (e2, e2_more), (e3,))):
            x = lax.rem(place[0] + d, NX)
            for z in range(NZ):
                at = pl.ds(pl.multiple_of((NX * z + x) * 64, 64), 64)
                eh[at, :], el[at, :] = halves(part[z * len(part) // NZ][z % (NZ // len(part))])
        us[...] = jnp.zeros_like(us)
        u = both[0, : 4 * NY]
        for r in range(1, NX * NZ):
            u += both[r, : 4 * NY]
        for n in range(2 * NY):
            us[:2, n * 128 : (n + 1) * 128] = u[2 * n : 2 * n + 2]
            v[n] = jnp.concatenate([both[2 * n + k, 4 * NY :, :64] for k in range(2)], 1)

    blocks = [t[n] for n in range(2 * NY)]
    sums = []
    for w in range(2):
        total = blocks[0] * v[0, w : w + 1, :]
        for n in range(1, 2 * NY):
            total += blocks[n] * v[n, w : w + 1, :]
        th, tl = halves(total)
        ones = jnp.ones((PAD, 128), jnp.bfloat16)
        lanes = ((1,), (1,))
        sums.append((dot(ones, th, lanes) + dot(ones, tl, lanes))[:1])
    cols[...] = jnp.concatenate(sums, 0)
    th, tl = halves(jnp.concatenate([jnp.concatenate(blocks, 1), us[...]], 0))
    out = dot(th, eh[...]) + (dot(tl, eh[...]) + dot(th, el[...]))
    main[...] = out[:STEP]
    rows[...] = out[STEP : STEP + 2]


def product(place, t, parts, both):
    blocks, m, wide = t.shape
    whole = lambda a: pl.BlockSpec(a.shape, lambda i, s: (0,) * a.ndim)
    depth = blocks * wide
    return pl.pallas_call(
        product_kernel,
        out_shape=(
            jax.ShapeDtypeStruct((m, 256), jnp.float32),
            jax.ShapeDtypeStruct((2, 256), jnp.float32),
            jax.ShapeDtypeStruct((2, m), jnp.float32),
        ),
        grid_spec=pltpu.PrefetchScalarGridSpec(
            num_scalar_prefetch=1,
            grid=(m // STEP,),
            in_specs=[pl.BlockSpec((blocks, STEP, wide), lambda i, s: (0, i, 0))]
            + [whole(a) for a in (*parts, both)],
            out_specs=[
                pl.BlockSpec((STEP, 256), lambda i, s: (i, 0)),
                pl.BlockSpec((2, 256), lambda i, s: (0, 0)),
                pl.BlockSpec((2, STEP), lambda i, s: (0, i)),
            ],
            scratch_shapes=[pltpu.VMEM((depth, 256), jnp.bfloat16)] * 2
            + [pltpu.VMEM((PAD, depth), jnp.float32), pltpu.VMEM((blocks, 2, wide), jnp.float32)],
        ),
        compiler_params=pltpu.CompilerParams(vmem_limit_bytes=VMEM),
    )(place, t, *parts, both)


def to_all(value, axis, count, groups=None):
    copies = jnp.broadcast_to(value[None], (count,) + value.shape)
    return lax.all_to_all(copies, axis, split_axis=0, concat_axis=0, axis_index_groups=groups)


def on_device(transfer, emissions):
    highest = lax.Precision.HIGHEST
    row, col = lax.axis_index("row"), lax.axis_index("col")
    x = lax.rem(row, NX)
    m_local, s_local = transfer.shape[0], emissions.shape[1]
    whole = lax.all_gather(transfer, "col", axis=0)

    near = to_all(emissions, "row", NZ, Z_GROUPS)
    after, before = [lax.ppermute(near, "row", from_x(d)) for d in (1, 3)]

    receptor = check_weights(m_local * lax.axis_size("row"), row * m_local, m_local)
    u = jnp.dot(receptor, transfer, precision=highest, preferred_element_type=jnp.float32)
    scenario = check_weights(s_local * lax.axis_size("col"), col * s_local, s_local)
    v = jnp.einsum("js,ks->jk", scenario, emissions, precision=highest, preferred_element_type=jnp.float32)
    small = jnp.concatenate([u, v, jnp.zeros_like(v)], 1)
    small, near = lax.optimization_barrier((small, near))
    both = to_all(small, "col", 2 * NY)
    both = jnp.concatenate([both[:, :, :128], both[:, :, 128:].sum(0)[None]], 0)
    both, after, before = lax.optimization_barrier((both, after, before))
    both = to_all(both.reshape(-1, both.shape[-1]), "row", NX * NZ)

    two = [
        lax.ppermute(after[: NZ // 2], "row", from_x(1)),
        lax.ppermute(before[NZ // 2 :], "row", from_x(3)),
    ]
    parts = [near, after, *two, before]

    place = jnp.stack([x]).astype(jnp.int32)
    return tuple(product(place, whole, parts, both))


def solution(mesh):
    placed = (P("row", "col"), P("row", "col"))
    return jax.shard_map(
        on_device,
        mesh=mesh,
        in_specs=placed,
        out_specs=(P("row", "col"), P(None, "col"), P(None, "row")),
        check_vma=False,
    )
```

```python
import jax
import jax.numpy as jnp
from jax import lax
from jax.experimental import pallas as pl
from jax.experimental.pallas import tpu as pltpu
from jax.sharding import PartitionSpec as P

NX, NY, NZ = 4, 8, 8
STEP = 256
PAD = 16
VMEM = 48 * 1024 * 1024

Z_GROUPS = [[NX * z + x for z in range(NZ)] for x in range(NX)]


def from_x(dx):
    return [(NX * z + (x + dx) % NX, NX * z + x) for z in range(NZ) for x in range(NX)]


def check_weights(total, start, count):
    index = (start + jnp.arange(count, dtype=jnp.int32)).astype(jnp.float32)
    flat = jnp.full((count,), 1.0, jnp.float32) / jnp.sqrt(jnp.float32(total))
    ramp = (index + 0.5) / total * jnp.sqrt(jnp.float32(3.0) / total)
    return jnp.stack([flat, ramp], 0)


def halves(value):
    high = value.astype(jnp.bfloat16)
    return high, (value - high.astype(jnp.float32)).astype(jnp.bfloat16)


def dot(left, right, contract=((1,), (0,))):
    return lax.dot_general(left, right, (contract, ((), ())), preferred_element_type=jnp.float32)


def product_kernel(place, t, e0, e1, e2, e2_more, e3, both, main, rows, cols, eh, el, us, v):
    @pl.when(pl.program_id(0) == 0)
    def _():
        for d, part in enumerate(((e0,), (e1,), (e2, e2_more), (e3,))):
            x = lax.rem(place[0] + d, NX)
            for z in range(NZ):
                at = pl.ds(pl.multiple_of((NX * z + x) * 64, 64), 64)
                eh[at, :], el[at, :] = halves(part[z * len(part) // NZ][z % (NZ // len(part))])
        us[...] = jnp.zeros_like(us)
        u = both[0, : 2 * NY]
        for r in range(1, NX * NZ):
            u += both[r, : 2 * NY]
        for n in range(2 * NY):
            us[:2, n * 128 : (n + 1) * 128] = u[n]
            v[n] = jnp.concatenate([both[2 * n + k, 2 * NY, :, :64] for k in range(2)], 1)

    blocks = [t[n] for n in range(2 * NY)]
    sums = []
    for w in range(2):
        total = blocks[0] * v[0, w : w + 1, :]
        for n in range(1, 2 * NY):
            total += blocks[n] * v[n, w : w + 1, :]
        th, tl = halves(total)
        ones = jnp.ones((PAD, 128), jnp.bfloat16)
        lanes = ((1,), (1,))
        sums.append((dot(ones, th, lanes) + dot(ones, tl, lanes))[:1])
    cols[...] = jnp.concatenate(sums, 0)
    th, tl = halves(jnp.concatenate([jnp.concatenate(blocks, 1), us[...]], 0))
    out = dot(th, eh[...]) + (dot(tl, eh[...]) + dot(th, el[...]))
    main[...] = out[:STEP]
    rows[...] = out[STEP : STEP + 2]


def product(place, t, parts, both):
    blocks, m, wide = t.shape
    depth = blocks * wide
    return pl.pallas_call(
        product_kernel,
        out_shape=(
            jax.ShapeDtypeStruct((m, 256), jnp.float32),
            jax.ShapeDtypeStruct((2, 256), jnp.float32),
            jax.ShapeDtypeStruct((2, m), jnp.float32),
        ),
        grid_spec=pltpu.PrefetchScalarGridSpec(
            num_scalar_prefetch=1,
            grid=(m // STEP,),
            in_specs=[pl.BlockSpec((blocks, STEP, wide), lambda i, s: (0, i, 0))]
            + [pl.BlockSpec(memory_space=pltpu.VMEM)] * (len(parts) + 1),
            out_specs=[
                pl.BlockSpec((STEP, 256), lambda i, s: (i, 0)),
                pl.BlockSpec((2, 256), lambda i, s: (0, 0)),
                pl.BlockSpec((2, STEP), lambda i, s: (0, i)),
            ],
            scratch_shapes=[pltpu.VMEM((depth, 256), jnp.bfloat16)] * 2
            + [pltpu.VMEM((PAD, depth), jnp.float32), pltpu.VMEM((blocks, 2, wide), jnp.float32)],
        ),
        compiler_params=pltpu.CompilerParams(vmem_limit_bytes=VMEM),
    )(place, t, *parts, both)


def to_all(value, axis, count, groups=None):
    copies = jnp.broadcast_to(value[None], (count,) + value.shape)
    return lax.all_to_all(copies, axis, split_axis=0, concat_axis=0, axis_index_groups=groups)


def on_device(transfer, emissions):
    highest = lax.Precision.HIGHEST
    row, col = lax.axis_index("row"), lax.axis_index("col")
    x = lax.rem(row, NX)
    m_local, s_local = transfer.shape[0], emissions.shape[1]
    whole = lax.all_gather(transfer, "col", axis=0)

    near = to_all(emissions, "row", NZ, Z_GROUPS)
    after, before = [lax.ppermute(near, "row", from_x(d)) for d in (1, 3)]

    receptor = check_weights(m_local * lax.axis_size("row"), row * m_local, m_local)
    u = jnp.dot(receptor, transfer, precision=highest, preferred_element_type=jnp.float32)
    scenario = check_weights(s_local * lax.axis_size("col"), col * s_local, s_local)
    v = jnp.einsum("js,ks->jk", scenario, emissions, precision=highest, preferred_element_type=jnp.float32)
    small = jnp.concatenate([u, v, jnp.zeros_like(v)], 1)
    small, near = lax.optimization_barrier((small, near))
    both = to_all(small, "col", 2 * NY)
    both = jnp.concatenate([both[:, :, :128], both[:, :, 128:].sum(0)[None]], 0)
    both, after, before = lax.optimization_barrier((both, after, before))
    both = to_all(both, "row", NX * NZ)

    two = [
        lax.ppermute(after[: NZ // 2], "row", from_x(1)),
        lax.ppermute(before[NZ // 2 :], "row", from_x(3)),
    ]
    parts = [near, after, *two, before]

    place = jnp.stack([x]).astype(jnp.int32)
    return tuple(product(place, whole, parts, both))


def solution(mesh):
    placed = (P("row", "col"), P("row", "col"))
    return jax.shard_map(
        on_device,
        mesh=mesh,
        in_specs=placed,
        out_specs=(P("row", "col"), P(None, "col"), P(None, "row")),
        check_vma=False,
    )
```
